32 devices in a mesh: section: 2 (over x), dp: 4 (over y, core), tensor: 4 (over z).
Axes of the slice: x: 2, y: 2, z: 4, core: 2. Of those that a mesh axis runs over, the one named last changes fastest.
Arguments:
- boundary: bfloat16 [2, 4, 1024, 4, 640], P('section', None, 'tensor', 'dp'), may hold values from -6 to 6
- positions: int32 [4, 1024, 4], P(None, None, 'dp'), may hold values from 0 to 1023, as said below
- w_query: bfloat16 [2, 640, 1024], P('section', 'dp', 'tensor'), may hold values from -0.25 to 0.25
- w_keyval: bfloat16 [2, 640, 512], P('section', 'dp', 'tensor'), may hold values from -0.25 to 0.25
- w_out: bfloat16 [2, 1024, 640], P('section', 'tensor', 'dp'), may hold values from -0.1875 to 0.1875
- w_gateup: bfloat16 [2, 640, 2, 2048], P('section', 'dp', None, 'tensor'), may hold values from -0.25 to 0.25
- down_weight: bfloat16 [2, 2048, 640], P('section', 'tensor', 'dp'), may hold values from -0.125 to 0.125
- norm_gains: float32 [2, 4, 640], P('section'), may hold values from 0.1 to 1.9
- qk_gains: float32 [2, 2, 256], P('section'), may hold values from 0.1 to 1.9
Outputs:
- ends: float32 [2, 4, 1024, 4, 640], P('section', None, 'tensor', 'dp')
- grad_query: float32 [2, 640, 1024], P('section', 'dp', 'tensor')
- grad_keyval: float32 [2, 640, 512], P('section', 'dp', 'tensor')
- grad_out: float32 [2, 1024, 640], P('section', 'tensor', 'dp')
- grad_gateup: float32 [2, 640, 2, 2048], P('section', 'dp', None, 'tensor')
- grad_down: float32 [2, 2048, 640], P('section', 'tensor', 'dp')
- grad_norm_gains: float32 [2, 4, 640], P('section')
- grad_qk_gains: float32 [2, 2, 256], P('section')
The draws below stay inside these ranges and needn't reach their ends.
Inputs may be any that keep to these rules, and one draw needn't show every extreme that they name: `positions`: sequences are packed with whole documents in order; a document begins where the position is 0 (always at a sequence's first token) and counts up by one; every sequence holds one document of 832 tokens or more.
All inputs are finite; a program needn't handle non-finite values.
Results may differ from the reference program's by a relative error of at most 0.035.
Values may be sent and summed in bfloat16 or wider, within the bound.
A program may use at most 192 MiB of HBM per device.

```python
import jax
import jax.numpy as jnp
from jax import lax

D = 640
HEADS = 4
HD = 256
FF = 2048
WIN = 512
LEN = 1024
MB = 4
NSEQ = 4
N_SECTION = 2


def draw_positions(key, part):
    key = jax.random.fold_in(key, 7)
    first_key, second_key = jax.random.split(key)
    count = MB * NSEQ
    longest = jax.random.randint(first_key, (count,), 13 * LEN // 16, LEN + 1)
    longest = jnp.where(jnp.arange(count) == 0, LEN, longest)
    offset = jax.random.randint(second_key, (count,), 0, LEN - longest + 1)
    steps = jnp.arange(LEN)[None, :]
    begin = offset[:, None]
    finish = (offset + longest)[:, None]
    places = jnp.where(steps < begin, steps, jnp.where(steps < finish, steps - begin, steps - finish))
    return places.reshape(MB, NSEQ, LEN).transpose(0, 2, 1).astype(jnp.int32)


def shard_levels(own_key, dims, cuts, smallest, top_value):
    def one(position, shards_of):
        steps = jax.random.uniform(jax.random.fold_in(jax.random.fold_in(own_key, 6), position), (shards_of,), jnp.float32, smallest / len(cuts), top_value / len(cuts))
        return jnp.repeat(jnp.exp(steps), dims[position] // shards_of).reshape((-1,) + (1,) * (len(dims) - position - 1))

    loudness = one(*cuts[0])
    for cut in cuts[1:]:
        loudness = loudness * one(*cut)
    return loudness


def centred(own_key, shape, scale, bound, shards=(), held_as=jnp.bfloat16):
    values = jax.random.normal(own_key, shape, jnp.float32) * scale
    if len(shards) > 0:
        values = shard_levels(own_key, shape, shards, -0.22, 0.18) * values
    return jnp.clip(values, min=-bound, max=bound).astype(held_as)


def setup_inputs(seed: int = 0) -> dict:
    key_of = jax.random.split(jax.random.key(seed), 10)
    boundary = centred(key_of[0], (N_SECTION, MB, LEN, NSEQ, D), 1.0, 6.0, ((0, 2), (2, 4), (3, 4)))
    positions = draw_positions(jax.random.fold_in(key_of[9], 71), 0)
    w_query = centred(key_of[2], (N_SECTION, D, HEADS * HD), D ** -0.5, 0.25, ((0, 2), (1, 4), (2, 4)))
    w_keyval = centred(key_of[3], (N_SECTION, D, 2 * HD), D ** -0.5, 0.25, ((0, 2), (1, 4), (2, 4)))
    w_out = centred(key_of[4], (N_SECTION, HEADS * HD, D), (HEADS * HD) ** -0.5, 0.1875, ((0, 2), (1, 4), (2, 4)))
    w_gateup = centred(key_of[5], (N_SECTION, D, 2, FF), D ** -0.5, 0.25, ((0, 2), (1, 4), (3, 4)))
    down_weight = centred(key_of[6], (N_SECTION, FF, D), FF ** -0.5, 0.125, ((0, 2), (1, 4), (2, 4)))
    norm_gains = jnp.clip(1.0 + 0.18 * jax.random.normal(key_of[7], (N_SECTION, 4, D), jnp.float32), 0.1, 1.9)
    qk_gains = jnp.clip(1.0 + 0.18 * jax.random.normal(key_of[8], (N_SECTION, 2, HD), jnp.float32), 0.1, 1.9)
    return dict(boundary=boundary, positions=positions, w_query=w_query, w_keyval=w_keyval, w_out=w_out, w_gateup=w_gateup, down_weight=down_weight, norm_gains=norm_gains, qk_gains=qk_gains)


@jax.custom_vjp
def low(v):
    return lax.optimization_barrier(v.astype(jnp.bfloat16)).astype(jnp.float32)

@jax.custom_vjp
def low_back(v):
    return v

def low_keep(v):
    return (low(v), None)

def low_pass(kept, grad):
    return (grad,)

def back_keep(v):
    return (v, None)

def back_low(kept, grad):
    return (low(grad),)
low.defvjp(low_keep, low_pass)
low_back.defvjp(back_keep, back_low)
epsilon = 1e-06
highest = lax.Precision.HIGHEST

def rms_scale(rows, gain):
    return rows * lax.rsqrt(lax.optimization_barrier(jnp.mean(rows * rows, axis=-1, keepdims=True)) + epsilon) * gain

def rotary_angles(places, base, width):
    freqs = jnp.exp(-jnp.log(base) * jnp.arange(width // 2, dtype=jnp.float32) * (2.0 / width))
    return places.astype(jnp.float32)[..., None] * freqs

def rotary(values, angles):
    half = values.shape[-1] // 2
    front, back = (values[..., :half], values[..., half:])
    cosine, sine = (jnp.cos(angles), jnp.sin(angles))
    return jnp.concatenate([front * cosine - back * sine, back * cosine + front * sine], axis=-1)

def attend(query, keys, values, places, window):
    group, length = (query.shape[0], query.shape[1])
    block = min(512, length)
    count = length // block
    documents = jnp.cumsum((places == 0).astype(jnp.int32), axis=1)
    scale = query.shape[-1] ** (-0.5)

    def one_block(args):
        query_block, block_pos, block_doc = args
        scores = low_back(jnp.einsum('gqhd,gkd->ghqk', query_block, keys, precision=highest) * scale)
        allowed = (block_doc[:, :, None] == documents[:, None, :]) & (places[:, None, :] <= block_pos[:, :, None]) & (block_pos[:, :, None] - places[:, None, :] < window)
        scores = jnp.where(allowed[:, None], scores, -1e+30)
        probs = low(jax.nn.softmax(scores, axis=-1))
        return jnp.einsum('ghqk,gkd->gqhd', probs, values, precision=highest)
    query_blocks = query.reshape((group, count, block) + query.shape[2:]).transpose(1, 0, 2, 3, 4)
    pos_blocks = places.reshape(group, count, block).transpose(1, 0, 2)
    doc_blocks = documents.reshape(group, count, block).transpose(1, 0, 2)
    mixed = lax.map(jax.checkpoint(one_block), (query_blocks, pos_blocks, doc_blocks))
    return mixed.transpose(1, 0, 2, 3, 4).reshape(group, length, -1)

def layer(rows, weights, places, window, base):
    w_query, w_keyval, w_out, w_gateup, down_weight, gains, qk_gain = weights
    group, length = (rows.shape[0], rows.shape[1])
    normed = low(rms_scale(rows, gains[0]))
    query_raw = low_back(jnp.einsum('gld,de->gle', normed, w_query, precision=highest)).reshape(group, length, HEADS, HD)
    keyval = low(low_back(jnp.einsum('gld,de->gle', normed, w_keyval, precision=highest)))
    angles = rotary_angles(places, base, HD)
    query = low(rotary(rms_scale(query_raw, qk_gain[0]), angles[:, :, None]))
    keys = low(rotary(rms_scale(keyval[..., :HD], qk_gain[1]), angles))
    mixed = low(low_back(attend(query, keys, keyval[..., HD:], places, window)))
    branch = low_back(jnp.einsum('gle,ed->gld', mixed, w_out, precision=highest))
    middle = rows + rms_scale(branch, gains[1])
    normed_ff = low(rms_scale(middle, gains[2]))
    gateup = low_back(jnp.einsum('gld,dkf->glkf', normed_ff, w_gateup, precision=highest))
    hidden_state = low(jax.nn.gelu(gateup[:, :, 0], approximate=True) * gateup[:, :, 1])
    feedforward_branch = low_back(jnp.einsum('glf,fd->gld', hidden_state, down_weight, precision=highest))
    return middle + rms_scale(feedforward_branch, gains[3])

def reference(boundary, positions, w_query, w_keyval, w_out, w_gateup, down_weight, norm_gains, qk_gains):
    total = MB * NSEQ

    def arrange(array):
        return array.astype(jnp.float32).transpose(0, 2, 1, 3).reshape(total // 4, 4, LEN, D)
    inputs = arrange(boundary[0])
    cotangents = arrange(boundary[1])
    places = positions.transpose(0, 2, 1).reshape(total // 4, 4, LEN)
    params = tuple((array.astype(jnp.float32) for array in (w_query, w_keyval, w_out, w_gateup, down_weight, norm_gains, qk_gains)))

    def forward(rows, weights, places_group):
        first = layer(rows, tuple((array[0] for array in weights)), places_group, WIN, 10000.0)
        passed = low_back(low(first))
        return layer(passed, tuple((array[1] for array in weights)), places_group, LEN + 1, 1000000.0)

    def step(totals, item):
        rows, cotangent, places_group = item
        output, pull = jax.vjp(lambda given, weights: forward(given, weights, places_group), rows, params)
        grad_rows, grad_weights = pull(cotangent)
        return (jax.tree.map(jnp.add, totals, grad_weights), (output, grad_rows))
    zeros = jax.tree.map(jnp.zeros_like, params)
    totals, (outputs, grad_inputs) = lax.scan(step, zeros, (inputs, cotangents, places))

    def restore(array):
        return array.reshape(MB, NSEQ, LEN, D).transpose(0, 2, 1, 3)
    ends = jnp.stack([restore(grad_inputs), restore(outputs)])
    return (ends, totals[0], totals[1], totals[2], totals[3], totals[4], totals[5], totals[6])
```

```python
import jax
import jax.numpy as jnp
from jax import lax
from jax.sharding import PartitionSpec as P

HD = 256
WIN = 512

BASES = (10000.0, 1000000.0)
EPS = 1e-06
EVERY = ("tensor", "dp", "section")
BF = jnp.bfloat16
F32 = jnp.float32


def dots(pattern, left, right):
    return jnp.einsum(pattern, left, right, preferred_element_type=F32)


def swap(array):
    return lax.ppermute(array, "section", [(0, 1), (1, 0)])


def rms_scale(rows, gain):
    return rows * lax.rsqrt(jnp.mean(rows * rows, axis=-1, keepdims=True) + EPS) * gain


def rotary_tables(places, base):
    freqs = jnp.exp(-jnp.log(jnp.float32(base)) * jnp.arange(HD // 2, dtype=F32) * (2.0 / HD))
    angles = places.astype(F32)[:, None] * freqs
    return jnp.cos(angles), jnp.sin(angles)


def rotated(values, gain, tables):
    cosine, sine = tables
    values = rms_scale(values, gain)
    front, back = values[..., : HD // 2], values[..., HD // 2 :]
    return jnp.concatenate([front * cosine - back * sine, back * cosine + front * sine], axis=-1)


def gated(gate, up):
    return jax.nn.gelu(gate, approximate=True) * up


def layer_forward(rows, attn_weights, ff_weights, gains, qk_gain, tables, mask):
    w_query, w_keyval, w_out = attn_weights
    w_gateup, w_down = ff_weights
    heads = w_query.shape[0]
    length = rows.shape[0]
    normed = rms_scale(rows, gains[0]).astype(BF)
    keyval = dots("ld,tdc->ltc", normed, w_keyval).reshape(length, 2 * HD).astype(BF)
    keys_raw = keyval[:, :HD].astype(F32)
    own = jnp.concatenate([rotated(keys_raw, qk_gain[1], tables).astype(BF), keyval[:, HD:]], axis=1)
    both = jnp.concatenate([own, swap(own)], axis=0)
    keys, values = both[:, :HD], both[:, HD:]
    query_raw = dots("ld,tdc->tlc", normed, w_query)
    query = rotated(query_raw, qk_gain[0], tables).astype(BF)
    scores = dots("hqd,kd->hqk", query, keys) * (HD ** -0.5)
    scores = jnp.where(mask[None], scores, -1e30)
    peak = jnp.max(scores, axis=-1, keepdims=True)
    weights = jnp.exp(scores - peak)
    probs = (weights / jnp.sum(weights, axis=-1, keepdims=True)).astype(BF)
    mixed = dots("hqk,kd->hqd", probs, values).astype(BF)
    branch = dots("hqe,hde->qd", mixed, w_out)
    middle = rows + rms_scale(branch, gains[1])
    normed_ff = rms_scale(middle, gains[2]).astype(BF)
    gateup = dots("ld,tdc->tlc", normed_ff, w_gateup)
    half = gateup.shape[-1] // 2
    hidden = gated(gateup[..., :half], gateup[..., half:]).astype(BF)
    branch_ff = dots("tlf,tdf->ld", hidden, w_down)
    output = middle + rms_scale(branch_ff, gains[3])
    kept = (rows, normed, keys_raw, query_raw, query, keys, values, probs, mixed, branch, middle,
            normed_ff, gateup, hidden, branch_ff)
    return output, kept


def layer_backward(kept, attn_weights, ff_weights, gains, qk_gain, tables, grad_output):
    (rows, normed, keys_raw, query_raw, query, keys, values, probs, mixed, branch, middle,
     normed_ff, gateup, hidden, branch_ff) = kept
    w_query, w_keyval, w_out = attn_weights
    w_gateup, w_down = ff_weights
    length = rows.shape[0]
    parts = w_query.shape[0]
    _, pull = jax.vjp(rms_scale, branch_ff, gains[3])
    d_branch_ff, dg3 = pull(grad_output)
    d_branch_ff = d_branch_ff.astype(BF)
    d_hidden = dots("ld,tdf->tlf", d_branch_ff, w_down)
    g_down = dots("ld,tlf->tdf", d_branch_ff, hidden).astype(BF)
    half = gateup.shape[-1] // 2
    _, pull = jax.vjp(gated, gateup[..., :half], gateup[..., half:])
    d_gate, d_up = pull(d_hidden)
    d_gateup = jnp.concatenate([d_gate.astype(BF), d_up.astype(BF)], axis=-1)
    g_gateup = dots("ld,tlc->tdc", normed_ff, d_gateup).astype(BF)
    ff_share = scatter_total((g_gateup, g_down))
    d_normed_ff = dots("tlc,tdc->ld", d_gateup, w_gateup)
    _, pull = jax.vjp(rms_scale, middle, gains[2])
    d_middle, dg2 = pull(d_normed_ff)
    d_middle = d_middle + grad_output
    _, pull = jax.vjp(rms_scale, branch, gains[1])
    d_branch, dg1 = pull(d_middle)
    d_branch = d_branch.astype(BF)
    d_mixed = dots("qd,hde->hqe", d_branch, w_out).astype(BF)
    g_out = dots("qd,hqe->hde", d_branch, mixed).astype(BF)
    d_probs = dots("hqd,kd->hqk", d_mixed, values)
    wide = probs.astype(F32)
    inner = jnp.sum(wide * d_probs, axis=-1, keepdims=True)
    d_scores = (wide * (d_probs - inner)).astype(BF)
    scale = HD ** -0.5
    d_keys = dots("hqk,hqd->kd", d_scores, query) * scale
    d_values = dots("hqk,hqd->kd", probs, d_mixed)
    d_both = jnp.concatenate([d_keys, d_values], axis=1)
    arrived = swap(d_both[length:].astype(BF))
    d_query = dots("hqk,kd->hqd", d_scores, keys) * scale
    _, pull = jax.vjp(lambda raw, gain: rotated(raw, gain, tables), query_raw, qk_gain[0])
    d_query_raw, dgq = pull(d_query)
    d_query_raw = d_query_raw.astype(BF)
    d_both = d_both[:length] + arrived.astype(F32)
    _, pull = jax.vjp(lambda raw, gain: rotated(raw, gain, tables), keys_raw, qk_gain[1])
    d_keys_raw, dgk = pull(d_both[:, :HD])
    d_keyval = jnp.concatenate([d_keys_raw, d_both[:, HD:]], axis=1).astype(BF)
    d_keyval = d_keyval.reshape(length, parts, 2 * HD // parts)
    g_query = dots("ld,tlc->tdc", normed, d_query_raw).astype(BF)
    g_keyval = dots("ld,ltc->tdc", normed, d_keyval).astype(BF)
    attn_share = scatter_total((g_query, g_keyval, g_out))
    d_normed = dots("tlc,tdc->ld", d_query_raw, w_query) + dots("ltc,tdc->ld", d_keyval, w_keyval)
    _, pull = jax.vjp(rms_scale, rows, gains[0])
    d_rows, dg0 = pull(d_normed)
    d_rows = d_rows + d_middle
    small = jnp.concatenate([dg0, dg1, dg2, dg3, dgq, dgk])
    return d_rows, attn_share, ff_share, small


def gathered(shard, widths):
    tensor = lax.axis_size("tensor")
    whole = lax.all_gather(shard, EVERY, axis=0, tiled=True)
    whole = whole.reshape(tensor, whole.shape[0] // tensor, whole.shape[1])
    pieces, at = [], 0
    for width in widths:
        pieces.append(whole[:, :, at : at + width])
        at += width
    return tuple(pieces)


def scatter_total(grads):
    packed = jnp.concatenate(grads, axis=2)
    packed = packed.reshape(packed.shape[0] * packed.shape[1], packed.shape[2])
    return lax.psum_scatter(packed, EVERY, scatter_dimension=0, tiled=True)


def body(
    boundary, positions, w_query, w_keyval, w_out, w_gateup, down_weight, norm_gains, qk_gains
):
    section = lax.axis_index("section")
    first = section == 0
    tensor = lax.axis_size("tensor")
    local = boundary[0][:, :, 0]
    micro, span, width = local.shape
    part = span // 2

    attn = jnp.concatenate([w_query[0], w_keyval[0], w_out[0].T], axis=1)
    ff_in = w_gateup[0].reshape(w_gateup.shape[1], -1)
    ff = jnp.concatenate([ff_in, down_weight[0].T], axis=1)
    attn_widths = (w_query.shape[2], w_keyval.shape[2], w_out.shape[1])
    ff_widths = (ff_in.shape[1], down_weight.shape[1])
    packed = jnp.concatenate([attn, ff], axis=1)
    rows_half = packed.shape[0] // 2
    top, bottom = packed[:rows_half], packed[rows_half:]
    mine = jnp.where(first, top, bottom)
    other = swap(jnp.where(first, bottom, top))
    layers = (jnp.where(first, mine, other), jnp.where(first, other, mine))
    cut = attn.shape[1]
    attn_w = [None, None]
    ff_w = [None, None]
    for index in range(2):
        attn_w[index] = gathered(layers[index][:, :cut], attn_widths)
        ff_w[index] = gathered(layers[index][:, cut:], ff_widths)

    gains = lax.all_gather(
        jnp.concatenate([norm_gains[0].reshape(-1), qk_gains[0].reshape(-1)]), "section", axis=0
    )
    split = norm_gains.shape[1] * norm_gains.shape[2]
    norm_all = gains[:, :split].reshape(2, norm_gains.shape[1], norm_gains.shape[2])
    qk_all = gains[:, split:].reshape(2, 2, HD)

    sent = local.reshape(micro, 2, part, width).transpose(1, 0, 2, 3)
    sent = sent.reshape(2 * micro, part, width)
    came = lax.all_to_all(sent, ("section", "tensor"), 0, 0, tiled=True)
    rows = came[:micro].reshape(micro * part, width).astype(F32)
    cotangent = came[micro:].reshape(micro * part, width).astype(F32)

    places = lax.dynamic_index_in_dim(
        positions[:, :, 0], lax.axis_index("tensor"), 0, keepdims=False
    )
    documents = jnp.cumsum((places == 0).astype(jnp.int32))

    def halves(values):
        values = values.reshape(micro, 2, part)
        even, odd = values[:, 0].reshape(-1), values[:, 1].reshape(-1)
        return jnp.where(first, even, odd), jnp.where(first, odd, even)

    own_pos, other_pos = halves(places)
    own_doc, other_doc = halves(documents)
    key_pos = jnp.concatenate([own_pos, other_pos])
    key_doc = jnp.concatenate([own_doc, other_doc])
    gap = own_pos[:, None] - key_pos[None, :]
    causal = (own_doc[:, None] == key_doc[None, :]) & (gap >= 0)
    masks = (causal & (gap < WIN), causal)
    tables = tuple(rotary_tables(own_pos, base) for base in BASES)

    kept = [None, None]
    for index in range(2):
        output, kept[index] = layer_forward(
            rows, attn_w[index], ff_w[index], norm_all[index], qk_all[index], tables[index],
            masks[index],
        )
        rows = output.astype(BF).astype(F32)
    grad = cotangent
    shares = [None, None]
    smalls = [None, None]
    for index in (1, 0):
        grad_rows, attn_share, ff_share, smalls[index] = layer_backward(
            kept[index], attn_w[index], ff_w[index], norm_all[index], qk_all[index],
            tables[index], grad,
        )
        shares[index] = jnp.concatenate([attn_share, ff_share], axis=1)
        grad = grad_rows.astype(BF).astype(F32)

    back = jnp.stack([grad_rows.astype(BF), output.astype(BF)]).reshape(2 * micro, part, width)
    back = lax.all_to_all(back, ("section", "tensor"), 0, 0, tiled=True)
    ends = back.reshape(2, micro, part, width).transpose(1, 0, 2, 3).reshape(micro, span, width)
    ends = ends.astype(F32)[None, :, :, None]

    passed = swap(jnp.where(first, shares[1], shares[0]))
    stayed = jnp.where(first, shares[0], shares[1])
    grads = jnp.concatenate(
        [jnp.where(first, stayed, passed), jnp.where(first, passed, stayed)], axis=0
    ).astype(F32)
    found, at = [], 0
    for size in attn_widths + ff_widths:
        found.append(grads[:, at : at + size])
        at += size
    small = lax.psum(jnp.stack(smalls), ("section", "dp", "tensor"))
    small = lax.dynamic_index_in_dim(small, section, 0, keepdims=False)
    return (
        ends,
        found[0][None],
        found[1][None],
        found[2].T[None],
        found[3].reshape(w_gateup.shape),
        found[4].T[None],
        small[:split].reshape(norm_gains.shape),
        small[split:].reshape(qk_gains.shape),
    )


def solution(mesh):
    in_specs = (
        P("section", None, "tensor", "dp", None),
        P(None, None, "dp"),
        P("section", "dp", "tensor"),
        P("section", "dp", "tensor"),
        P("section", "tensor", "dp"),
        P("section", "dp", None, "tensor"),
        P("section", "tensor", "dp"),
        P("section", None, None),
        P("section", None, None),
    )
    out_specs = (
        P("section", None, "tensor", "dp", None),
        P("section", "dp", "tensor"),
        P("section", "dp", "tensor"),
        P("section", "tensor", "dp"),
        P("section", "dp", None, "tensor"),
        P("section", "tensor", "dp"),
        P("section", None, None),
        P("section", None, None),
    )
    return jax.shard_map(body, mesh=mesh, in_specs=in_specs, out_specs=out_specs, check_vma=False)
```

```python
import jax
import jax.numpy as jnp
from jax import lax
from jax.experimental import pallas as pl
from jax.experimental.pallas import tpu as pltpu
from jax.sharding import PartitionSpec as P

HD = 256
WIN = 512

BASES = (10000.0, 1000000.0)
EPS = 1e-06
EVERY = ("tensor", "dp", "section")
BF = jnp.bfloat16
F32 = jnp.float32


def dots(pattern, left, right):
    return jnp.einsum(pattern, left, right, preferred_element_type=F32)


def swap(array):
    return lax.ppermute(array, "section", [(0, 1), (1, 0)])


def rms_scale(rows, gain):
    return rows * lax.rsqrt(jnp.mean(rows * rows, axis=-1, keepdims=True) + EPS) * gain


def rotary_tables(places, base):
    freqs = jnp.exp(-jnp.log(jnp.float32(base)) * jnp.arange(HD // 2, dtype=F32) * (2.0 / HD))
    angles = places.astype(F32)[:, None] * freqs
    return jnp.cos(angles), jnp.sin(angles)


def rotated(values, gain, tables):
    cosine, sine = tables
    values = rms_scale(values, gain)
    front, back = values[..., : HD // 2], values[..., HD // 2 :]
    return jnp.concatenate([front * cosine - back * sine, back * cosine + front * sine], axis=-1)


def gated(gate, up):
    return jax.nn.gelu(gate, approximate=True) * up


def grads_kernel(normed, normed_ff, d_branch, d_branch_ff, d_query, d_keyval, mixed, d_gateup,
                 hidden, out):
    at = 0
    for left, right in (
        (normed, d_query.at[0]), (normed, d_keyval), (d_branch, mixed.at[0]),
        (normed_ff, d_gateup.at[0]), (d_branch_ff, hidden.at[0]),
    ):
        size = right.shape[1]
        product = lax.dot_general(
            left[...], right[...], (((0,), (0,)), ((), ())), preferred_element_type=F32
        )
        out[0, :, at : at + size] = product.astype(BF)
        at += size


def packed_grads(normed, normed_ff, d_branch, d_branch_ff, d_query, d_keyval, mixed, d_gateup,
                 hidden):
    parts, length = d_query.shape[:2]
    width = normed.shape[1]
    kv = d_keyval.shape[1] // parts
    columns = d_query.shape[2] + kv + mixed.shape[2] + d_gateup.shape[2] + hidden.shape[2]
    shared = pl.BlockSpec((length, width), lambda t: (0, 0))

    def own(array):
        return pl.BlockSpec((1, length, array.shape[2]), lambda t: (t, 0, 0))

    return pl.pallas_call(
        grads_kernel,
        grid=(parts,),
        out_shape=jax.ShapeDtypeStruct((parts, width, columns), BF),
        in_specs=[shared] * 4
        + [own(d_query), pl.BlockSpec((length, kv), lambda t: (0, t))]
        + [own(mixed), own(d_gateup), own(hidden)],
        out_specs=pl.BlockSpec((1, width, columns), lambda t: (t, 0, 0)),
        compiler_params=pltpu.CompilerParams(vmem_limit_bytes=40 * 1024 * 1024),
        cost_estimate=pl.CostEstimate(
            flops=2 * parts * length * width * columns,
            bytes_accessed=2 * parts * columns * (width + length) + 8 * length * width,
            transcendentals=0,
        ),
    )(normed, normed_ff, d_branch, d_branch_ff, d_query, d_keyval, mixed, d_gateup, hidden)


def layer_forward(rows, attn_weights, ff_weights, gains, qk_gain, tables, mask):
    w_query, w_keyval, w_out = attn_weights
    w_gateup, w_down = ff_weights
    heads = w_query.shape[0]
    length = rows.shape[0]
    normed = rms_scale(rows, gains[0]).astype(BF)
    keyval = dots("ld,tdc->ltc", normed, w_keyval).reshape(length, 2 * HD).astype(BF)
    keys_raw = keyval[:, :HD].astype(F32)
    own = jnp.concatenate([rotated(keys_raw, qk_gain[1], tables).astype(BF), keyval[:, HD:]], axis=1)
    both = jnp.concatenate([own, swap(own)], axis=0)
    keys, values = both[:, :HD], both[:, HD:]
    query_raw = dots("ld,tdc->tlc", normed, w_query)
    query = rotated(query_raw, qk_gain[0], tables).astype(BF)
    scores = dots("hqd,kd->hqk", query, keys) * (HD ** -0.5)
    scores = jnp.where(mask[None], scores, -1e30)
    peak = jnp.max(scores, axis=-1, keepdims=True)
    weights = jnp.exp(scores - peak)
    probs = (weights / jnp.sum(weights, axis=-1, keepdims=True)).astype(BF)
    mixed = dots("hqk,kd->hqd", probs, values).astype(BF)
    branch = dots("hqe,hde->qd", mixed, w_out)
    middle = rows + rms_scale(branch, gains[1])
    normed_ff = rms_scale(middle, gains[2]).astype(BF)
    gateup = dots("ld,tdc->tlc", normed_ff, w_gateup)
    half = gateup.shape[-1] // 2
    hidden = gated(gateup[..., :half], gateup[..., half:]).astype(BF)
    branch_ff = dots("tlf,tdf->ld", hidden, w_down)
    output = middle + rms_scale(branch_ff, gains[3])
    kept = (rows, normed, keys_raw, query_raw, query, keys, values, probs, mixed, branch, middle,
            normed_ff, gateup, hidden, branch_ff)
    return output, kept


def layer_backward(kept, attn_weights, ff_weights, gains, qk_gain, tables, grad_output):
    (rows, normed, keys_raw, query_raw, query, keys, values, probs, mixed, branch, middle,
     normed_ff, gateup, hidden, branch_ff) = kept
    w_query, w_keyval, w_out = attn_weights
    w_gateup, w_down = ff_weights
    length = rows.shape[0]
    parts = w_query.shape[0]
    _, pull = jax.vjp(rms_scale, branch_ff, gains[3])
    d_branch_ff, dg3 = pull(grad_output)
    d_branch_ff = d_branch_ff.astype(BF)
    d_hidden = dots("ld,tdf->tlf", d_branch_ff, w_down)
    half = gateup.shape[-1] // 2
    _, pull = jax.vjp(gated, gateup[..., :half], gateup[..., half:])
    d_gate, d_up = pull(d_hidden)
    d_gateup = jnp.concatenate([d_gate.astype(BF), d_up.astype(BF)], axis=-1)
    d_normed_ff = dots("tlc,tdc->ld", d_gateup, w_gateup)
    _, pull = jax.vjp(rms_scale, middle, gains[2])
    d_middle, dg2 = pull(d_normed_ff)
    d_middle = d_middle + grad_output
    _, pull = jax.vjp(rms_scale, branch, gains[1])
    d_branch, dg1 = pull(d_middle)
    d_branch = d_branch.astype(BF)
    d_mixed = dots("qd,hde->hqe", d_branch, w_out).astype(BF)
    d_probs = dots("hqd,kd->hqk", d_mixed, values)
    wide = probs.astype(F32)
    inner = jnp.sum(wide * d_probs, axis=-1, keepdims=True)
    d_scores = (wide * (d_probs - inner)).astype(BF)
    scale = HD ** -0.5
    d_keys = dots("hqk,hqd->kd", d_scores, query) * scale
    d_values = dots("hqk,hqd->kd", probs, d_mixed)
    d_both = jnp.concatenate([d_keys, d_values], axis=1)
    arrived = swap(d_both[length:].astype(BF))
    d_query = dots("hqk,kd->hqd", d_scores, keys) * scale
    _, pull = jax.vjp(lambda raw, gain: rotated(raw, gain, tables), query_raw, qk_gain[0])
    d_query_raw, dgq = pull(d_query)
    d_query_raw = d_query_raw.astype(BF)
    d_both = d_both[:length] + arrived.astype(F32)
    _, pull = jax.vjp(lambda raw, gain: rotated(raw, gain, tables), keys_raw, qk_gain[1])
    d_keys_raw, dgk = pull(d_both[:, :HD])
    d_keyval = jnp.concatenate([d_keys_raw, d_both[:, HD:]], axis=1).astype(BF)
    packed = packed_grads(
        normed, normed_ff, d_branch, d_branch_ff, d_query_raw, d_keyval, mixed, d_gateup, hidden
    )
    d_keyval = d_keyval.reshape(length, parts, 2 * HD // parts)
    d_normed = dots("tlc,tdc->ld", d_query_raw, w_query) + dots("ltc,tdc->ld", d_keyval, w_keyval)
    _, pull = jax.vjp(rms_scale, rows, gains[0])
    d_rows, dg0 = pull(d_normed)
    d_rows = d_rows + d_middle
    small = jnp.concatenate([dg0, dg1, dg2, dg3, dgq, dgk])
    return d_rows, packed, small


def gathered(shard, widths):
    tensor = lax.axis_size("tensor")
    whole = lax.all_gather(shard, EVERY, axis=0, tiled=True)
    whole = whole.reshape(tensor, whole.shape[0] // tensor, whole.shape[1])
    pieces, at = [], 0
    for width in widths:
        pieces.append(whole[:, :, at : at + width])
        at += width
    return tuple(pieces)


def scatter_total(packed):
    packed = packed.reshape(packed.shape[0] * packed.shape[1], packed.shape[2])
    return lax.psum_scatter(packed, EVERY, scatter_dimension=0, tiled=True)


def body(
    boundary, positions, w_query, w_keyval, w_out, w_gateup, down_weight, norm_gains, qk_gains
):
    section = lax.axis_index("section")
    first = section == 0
    tensor = lax.axis_size("tensor")
    local = boundary[0][:, :, 0]
    micro, span, width = local.shape
    part = span // 2

    attn = jnp.concatenate([w_query[0], w_keyval[0], w_out[0].T], axis=1)
    ff_in = w_gateup[0].reshape(w_gateup.shape[1], -1)
    ff = jnp.concatenate([ff_in, down_weight[0].T], axis=1)
    attn_widths = (w_query.shape[2], w_keyval.shape[2], w_out.shape[1])
    ff_widths = (ff_in.shape[1], down_weight.shape[1])
    packed = jnp.concatenate([attn, ff], axis=1)
    rows_half = packed.shape[0] // 2
    top, bottom = packed[:rows_half], packed[rows_half:]
    mine = jnp.where(first, top, bottom)
    other = swap(jnp.where(first, bottom, top))
    layers = (jnp.where(first, mine, other), jnp.where(first, other, mine))
    first_w = gathered(layers[0], attn_widths + ff_widths)
    second_shard, _ = lax.optimization_barrier((layers[1], first_w[0]))
    second_w = gathered(second_shard, attn_widths + ff_widths)
    attn_w = (first_w[:3], second_w[:3])
    ff_w = (first_w[3:], second_w[3:])

    gains = lax.all_gather(
        jnp.concatenate([norm_gains[0].reshape(-1), qk_gains[0].reshape(-1)]), "section", axis=0
    )
    split = norm_gains.shape[1] * norm_gains.shape[2]
    norm_all = gains[:, :split].reshape(2, norm_gains.shape[1], norm_gains.shape[2])
    qk_all = gains[:, split:].reshape(2, 2, HD)

    sent = local.reshape(micro, 2, part, width).transpose(1, 0, 2, 3)
    sent = sent.reshape(2 * micro, part, width)
    came = lax.all_to_all(sent, ("section", "tensor"), 0, 0, tiled=True)
    rows = came[:micro].reshape(micro * part, width).astype(F32)
    cotangent = came[micro:].reshape(micro * part, width).astype(F32)

    places = lax.dynamic_index_in_dim(
        positions[:, :, 0], lax.axis_index("tensor"), 0, keepdims=False
    )
    documents = jnp.cumsum((places == 0).astype(jnp.int32))

    def halves(values):
        values = values.reshape(micro, 2, part)
        even, odd = values[:, 0].reshape(-1), values[:, 1].reshape(-1)
        return jnp.where(first, even, odd), jnp.where(first, odd, even)

    own_pos, other_pos = halves(places)
    own_doc, other_doc = halves(documents)
    key_pos = jnp.concatenate([own_pos, other_pos])
    key_doc = jnp.concatenate([own_doc, other_doc])
    gap = own_pos[:, None] - key_pos[None, :]
    causal = (own_doc[:, None] == key_doc[None, :]) & (gap >= 0)
    masks = (causal & (gap < WIN), causal)
    tables = tuple(rotary_tables(own_pos, base) for base in BASES)

    kept = [None, None]
    for index in range(2):
        output, kept[index] = layer_forward(
            rows, attn_w[index], ff_w[index], norm_all[index], qk_all[index], tables[index],
            masks[index],
        )
        rows = output.astype(BF).astype(F32)
    grad = cotangent
    shares = [None, None]
    smalls = [None, None]
    for index in (1, 0):
        grad_rows, packed_grad, smalls[index] = layer_backward(
            kept[index], attn_w[index], ff_w[index], norm_all[index], qk_all[index],
            tables[index], grad,
        )
        grad = grad_rows.astype(BF).astype(F32)
        if index == 1:
            grad, packed_grad = lax.optimization_barrier((grad, packed_grad))
        shares[index] = scatter_total(packed_grad)

    small = lax.psum(jnp.stack(smalls), ("section", "dp", "tensor"))
    sending, small = lax.optimization_barrier((grad_rows.astype(BF), small))
    back = jnp.stack([sending, output.astype(BF)]).reshape(2 * micro, part, width)
    back = lax.all_to_all(back, ("section", "tensor"), 0, 0, tiled=True)
    ends = back.reshape(2, micro, part, width).transpose(1, 0, 2, 3).reshape(micro, span, width)
    ends = ends.astype(F32)[None, :, :, None]

    passed = swap(jnp.where(first, shares[1], shares[0]))
    stayed = jnp.where(first, shares[0], shares[1])
    grads = jnp.concatenate(
        [jnp.where(first, stayed, passed), jnp.where(first, passed, stayed)], axis=0
    ).astype(F32)
    found, at = [], 0
    for size in attn_widths + ff_widths:
        found.append(grads[:, at : at + size])
        at += size
    small = lax.dynamic_index_in_dim(small, section, 0, keepdims=False)
    return (
        ends,
        found[0][None],
        found[1][None],
        found[2].T[None],
        found[3].reshape(w_gateup.shape),
        found[4].T[None],
        small[:split].reshape(norm_gains.shape),
        small[split:].reshape(qk_gains.shape),
    )


def solution(mesh):
    in_specs = (
        P("section", None, "tensor", "dp", None),
        P(None, None, "dp"),
        P("section", "dp", "tensor"),
        P("section", "dp", "tensor"),
        P("section", "tensor", "dp"),
        P("section", "dp", None, "tensor"),
        P("section", "tensor", "dp"),
        P("section", None, None),
        P("section", None, None),
    )
    out_specs = (
        P("section", None, "tensor", "dp", None),
        P("section", "dp", "tensor"),
        P("section", "dp", "tensor"),
        P("section", "tensor", "dp"),
        P("section", "dp", None, "tensor"),
        P("section", "tensor", "dp"),
        P("section", None, None),
        P("section", None, None),
    )
    return jax.shard_map(body, mesh=mesh, in_specs=in_specs, out_specs=out_specs, check_vma=False)
```
